512 devices in a mesh: dp: 32 (over z_hi, y, core), group: 16 (over z_lo, x).
Axes of the slice: x: 4, y: 8, z: 8 (z_hi: 2, z_lo: 4; z = z_hi * 4 + z_lo), core: 2. Of those that a mesh axis runs over, the one named last changes fastest.
Arguments:
- query_rows: bfloat16 [512, 384, 768], P(('dp', 'group')), may hold values from -24 to 24, as said below
- key_rows: bfloat16 [512, 384, 768], P(('dp', 'group')), may hold values from -24 to 24, as said below
- value_rows: bfloat16 [512, 384, 768], P(('dp', 'group')), may hold values from -6 to 6
- cotangent: bfloat16 [512, 384, 768], P(('dp', 'group')), may hold values from -6 to 6
- kept_counts: int32 [512], P(('dp', 'group')), may hold values from 92 to 380, as said below
- trades: int32 [512, 2], replicated, may hold values from 0 to 1
- layer_scale: float32 [768], replicated, may hold values from 0.1 to 1
Outputs:
- attended: bfloat16 [512, 384, 768], P(('dp', 'group'))
- query_grad: bfloat16 [512, 384, 768], P(('dp', 'group'))
- key_grad: bfloat16 [512, 384, 768], P(('dp', 'group'))
- value_grad: bfloat16 [512, 384, 768], P(('dp', 'group'))
- scale_grad: float32 [768], replicated
The draws below stay inside these ranges and needn't reach their ends.
Inputs may be any that keep to these rules, and one draw needn't show every extreme that they name: `kept_counts`: some image holds exactly 380 kept tokens. `query_rows`: entries are real numbers. `key_rows`: entries are real numbers.
All inputs are finite; a program needn't handle non-finite values.
Results may differ from the reference program's by a relative error of at most 0.025.
Values may be sent and summed in bfloat16 or wider, within the bound.
A program may use at most 64 MiB of HBM per device.

```python
import math
import jax
import jax.numpy as jnp
from jax import lax

HEAD_DIM = 64
WIDTH = 768
LT = 384
SLOTS = 1
ROUNDS = 2
IMAGES = 512
N_DP = 32
N_GROUP = 16


def draw_query_rows(key, part):
    key = jax.random.fold_in(key, 1)
    shape = (IMAGES, LT, WIDTH)
    rows = jnp.clip(jax.random.normal(key, shape, jnp.float32), -6.0, 6.0)
    return rows.astype(jnp.bfloat16)


def draw_key_rows(key, part):
    key = jax.random.fold_in(key, 2)
    shape = (IMAGES, LT, WIDTH)
    rows = jnp.clip(jax.random.normal(key, shape, jnp.float32), -6.0, 6.0)
    return rows.astype(jnp.bfloat16)


def draw_kept_counts(key, part):
    key = jax.random.fold_in(key, 3)
    counts = jax.random.randint(key, (IMAGES,), LT // 4 - 4, LT - 3, jnp.int32)
    return counts.at[0].set(LT - 4)


def place_ends(entries, key, smallest, largest):
    index_at = [jax.random.randint(jax.random.fold_in(key, axis), (), 0, length) for axis, length in enumerate(entries.shape)]
    widest = entries.shape.index(max(entries.shape))
    beside = index_at[:widest] + [(index_at[widest] + 1) % entries.shape[widest]] + index_at[widest + 1:]
    return entries.at[tuple(index_at)].set(smallest).at[tuple(beside)].set(largest)


def levels(stream_key, shape, pieces, least, top_value):
    level, own = 1.0, jax.random.fold_in(stream_key, 6)
    for position, shards_of in pieces:
        draws = jnp.exp(jax.random.uniform(jax.random.fold_in(own, position), (shards_of,), jnp.float32, least / len(pieces), top_value / len(pieces)))
        level = level * jnp.repeat(draws, shape[position] // shards_of).reshape([-1 if axis == position else 1 for axis in range(len(shape))])
    return level


def normal_values(rng, extent, scale, most, pieces=(), kind=jnp.bfloat16):
    level = levels(rng, extent, pieces, -0.22, 0.18) if pieces else 1.0
    entries = jax.random.normal(rng, extent, jnp.float32) * scale * level
    return jnp.minimum(jnp.maximum(entries, -most), most).astype(kind)


def setup_inputs(seed: int = 0) -> dict:
    streams_of = jax.random.split(jax.random.key(seed), 8)
    query_rows = draw_query_rows(jax.random.fold_in(streams_of[7], 71), 0)
    key_rows = draw_key_rows(jax.random.fold_in(streams_of[7], 71), 0)
    value_rows = normal_values(streams_of[2], (IMAGES, LT, WIDTH), 1.0, 6.0, ((0, 512),))
    cotangent = normal_values(streams_of[3], (IMAGES, LT, WIDTH), 1.0, 6.0, ((0, 512),))
    kept_counts = draw_kept_counts(jax.random.fold_in(streams_of[7], 71), 0)
    trades = place_ends(jax.random.randint(streams_of[5], (N_DP * N_GROUP, ROUNDS), 0, 2), jax.random.fold_in(streams_of[5], 1), 0, 1).astype(jnp.int32)
    layer_scale = jnp.clip(jnp.exp(jax.random.uniform(streams_of[6], (WIDTH,), jnp.float32, math.log(0.1), math.log(1.0))), 0.1, 1.0)
    return dict(query_rows=query_rows, key_rows=key_rows, value_rows=value_rows, cotangent=cotangent, kept_counts=kept_counts, trades=trades, layer_scale=layer_scale)


def attend_exact(query_rows, key_rows, value_rows, cotangent, kept_counts, layer_scale):
    slots, length, width = query_rows.shape
    heads = width // HEAD_DIM
    shape4 = (slots, length, heads, HEAD_DIM)
    high = lax.Precision.HIGHEST
    queries4 = query_rows.reshape(shape4).astype(jnp.float32)
    keys4 = key_rows.reshape(shape4).astype(jnp.float32)
    values4 = value_rows.reshape(shape4).astype(jnp.float32)
    factor = HEAD_DIM ** -0.5
    valid = jnp.arange(length, dtype=jnp.int32)[None, :] < (kept_counts + 4)[:, None]
    scores = jnp.einsum("sqhd,skhd->shqk", queries4, keys4, precision=high) * factor
    scores = jnp.where(valid[:, None, None, :], scores, -jnp.inf)
    top = jnp.max(scores, axis=-1, keepdims=True)
    expd = jnp.exp(scores - top)
    weights = expd / jnp.sum(expd, axis=-1, keepdims=True)
    weights_low = weights.astype(jnp.bfloat16)
    mixed = jnp.einsum("shqk,skhd->sqhd", weights_low.astype(jnp.float32), values4, precision=high).astype(jnp.bfloat16)
    mixed_rows = mixed.reshape(slots, length, width).astype(jnp.float32)
    row_mask = valid[:, :, None]
    attended = jnp.where(row_mask, layer_scale * mixed_rows, 0.0).astype(jnp.bfloat16)
    upstream = jnp.where(row_mask, cotangent.astype(jnp.float32) * layer_scale, 0.0).astype(jnp.bfloat16)
    scale_part = jnp.sum(jnp.where(row_mask, cotangent.astype(jnp.float32) * mixed_rows, 0.0), axis=(0, 1))
    upstream4 = upstream.reshape(shape4).astype(jnp.float32)
    delta = jnp.sum(upstream4 * mixed.astype(jnp.float32), axis=-1)
    delta = jnp.transpose(delta, (0, 2, 1))[..., None]
    weight_grad = jnp.einsum("sqhd,skhd->shqk", upstream4, values4, precision=high)
    score_grad = (weights * (weight_grad - delta) * factor).astype(jnp.bfloat16).astype(jnp.float32)
    query_grad = jnp.einsum("shqk,skhd->sqhd", score_grad, keys4, precision=high).astype(jnp.bfloat16)
    key_grad = jnp.einsum("shqk,sqhd->skhd", score_grad, queries4, precision=high).astype(jnp.bfloat16)
    value_grad = jnp.einsum("shqk,sqhd->skhd", weights_low.astype(jnp.float32), upstream4, precision=high).astype(jnp.bfloat16)
    return (attended, query_grad.reshape(slots, length, width), key_grad.reshape(slots, length, width),
            value_grad.reshape(slots, length, width), scale_part)


def reference(query_rows, key_rows, value_rows, cotangent, kept_counts, trades, layer_scale):
    devices_all = N_DP * N_GROUP
    group_bits = N_GROUP.bit_length() - 1
    holder = jnp.arange(IMAGES, dtype=jnp.int32)
    device_ids = jnp.arange(devices_all, dtype=jnp.int32)
    inside = device_ids % N_GROUP
    for round_index in range(ROUNDS):
        flip_bit = group_bits - 1 - round_index
        slot_pick = round_index % SLOTS
        partner = device_ids - inside + jnp.bitwise_xor(inside, 1 << flip_bit)
        lower = jnp.minimum(device_ids, partner)
        flag = trades[lower, round_index] == 1
        source = partner * SLOTS + slot_pick
        target = device_ids * SLOTS + slot_pick
        holder = holder.at[target].set(jnp.where(flag, holder[source], holder[target]))
    shape_blocks = (devices_all, SLOTS, LT, WIDTH)
    moved_q = query_rows[holder].reshape(shape_blocks)
    moved_k = key_rows[holder].reshape(shape_blocks)
    moved_v = value_rows[holder].reshape(shape_blocks)
    moved_c = cotangent.reshape(shape_blocks)
    moved_n = kept_counts[holder].reshape(devices_all, SLOTS)

    def one_block(items):
        return attend_exact(items[0], items[1], items[2], items[3], items[4], layer_scale)

    outs = lax.map(one_block, (moved_q, moved_k, moved_v, moved_c, moved_n))
    attended = outs[0].reshape(IMAGES, LT, WIDTH)
    query_grad = jnp.zeros((IMAGES, LT, WIDTH), jnp.bfloat16).at[holder].set(outs[1].reshape(IMAGES, LT, WIDTH))
    key_grad = jnp.zeros((IMAGES, LT, WIDTH), jnp.bfloat16).at[holder].set(outs[2].reshape(IMAGES, LT, WIDTH))
    value_grad = jnp.zeros((IMAGES, LT, WIDTH), jnp.bfloat16).at[holder].set(outs[3].reshape(IMAGES, LT, WIDTH))
    scale_grad = jnp.sum(outs[4], axis=0)
    return attended, query_grad, key_grad, value_grad, scale_grad
```

```python
import functools
import math

import jax
import jax.numpy as jnp
from jax import lax
from jax.experimental import pallas as pl
from jax.experimental.pallas import tpu as pltpu
from jax.sharding import PartitionSpec as P

MESH = pl.DeviceIdType.MESH
BF16 = jnp.bfloat16
F32 = jnp.float32
HEAD_DIM = 64
LANES = 128
FACTOR = HEAD_DIM ** -0.5
EXP_SCALE = FACTOR * math.log2(math.e)
PARTS = 3

NEAR, FAR = 4, 8


def flip(index, bit):
    return index + bit * (1 - 2 * ((index // bit) % 2))


def nt_dot(a, b):
    return lax.dot_general(a, b, (((1,), (1,)), ((), ())), preferred_element_type=F32)


def tn_dot(a, b):
    return lax.dot_general(a, b, (((0,), (0,)), ((), ())), preferred_element_type=F32)


def nn_dot(a, b):
    return jnp.dot(a, b, preferred_element_type=F32)


def sum_stages(dp_size):
    bits = [("group", 4), ("group", 8), ("group", 1), ("group", 2)]
    bit = 1
    while bit < dp_size:
        bits.append(("dp", bit))
        bit *= 2
    return [bits[i : i + 2] for i in range(0, len(bits), 2)]


def kernel(
    stages,
    q_hbm, k_hbm, v_hbm, c_hbm, count_ref, trades_ref, scale_ref,
    att_out, dq_out, dk_out, dv_out, sum_out,
    q, k, v, own_c, c_first, c_send, c_second, cot,
    att, a_first, a_send, a_second, att_final,
    weights, mixed, dq, dk, dv, part, sum_recv,
    load_sem, store_sem, send_sem, recv_sem, sum_send_sem, sum_recv_sem,
):
    g = lax.axis_index("group")
    d = lax.axis_index("dp")
    length, width = q.shape
    pairs = width // LANES
    half = length // 2
    rows = half // PARTS

    def peer(moves):
        pg, pd = g, d
        for axis, bit in moves:
            if axis == "group":
                pg = flip(pg, bit)
            else:
                pd = flip(pd, bit)
        return (pd, pg)

    def stage_peers(stage):
        if len(stage) == 1:
            return [[stage[0]]]
        return [[stage[0]], [stage[1]], [stage[0], stage[1]]]

    barrier = pltpu.get_barrier_semaphore()
    greeted = 0
    for stage in stages:
        for moves in stage_peers(stage):
            pl.semaphore_signal(barrier, inc=1, device_id=peer(moves), device_id_type=MESH)
            greeted += 1
    loads = [
        pltpu.make_async_copy(src.at[0], dst, load_sem.at[i])
        for i, (src, dst) in enumerate([(q_hbm, q), (k_hbm, k), (v_hbm, v), (c_hbm, own_c)])
    ]
    for copy in loads:
        copy.start()
    pl.semaphore_wait(barrier, greeted)

    a, b, x = g // 8, (g // 4) % 2, g % 4
    base = d * 16 + x

    def flag(offset, round_index):
        return trades_ref[round_index, base + offset] == 1

    far_mine, far_other = flag(b * 4, 0), flag((1 - b) * 4, 0)
    near_mine, near_other = flag(a * 8, 1), flag((1 - a) * 8, 1)
    near_at_source = jnp.logical_or(
        jnp.logical_and(far_mine, near_other),
        jnp.logical_and(jnp.logical_not(far_mine), near_mine),
    )
    far_at_source = jnp.logical_or(
        jnp.logical_and(near_mine, far_other),
        jnp.logical_and(jnp.logical_not(near_mine), far_mine),
    )

    def spans(part_index):
        return pl.ds(part_index * rows, rows), pl.ds(half + part_index * rows, rows)

    def remote(src, dst, bit, slot):
        return pltpu.make_async_remote_copy(
            src_ref=src, dst_ref=dst, send_sem=send_sem.at[slot], recv_sem=recv_sem.at[slot],
            device_id=peer([("group", bit)]), device_id_type=MESH,
        )

    c_hop1, c_hop2, a_hop1, a_hop2 = [], [], [], []
    for i in range(PARTS):
        top, low = spans(i)
        c_hop1.append((
            remote(c_hbm.at[0, top], c_first.at[top], NEAR, 8 * i),
            remote(c_hbm.at[0, low], c_first.at[low], FAR, 8 * i + 1),
        ))
        c_hop2.append((
            remote(c_send.at[top], c_second.at[top], FAR, 8 * i + 2),
            remote(c_send.at[low], c_second.at[low], NEAR, 8 * i + 3),
        ))
        a_hop1.append((
            remote(att.at[top], a_first.at[top], FAR, 8 * i + 4),
            remote(att.at[low], a_first.at[low], NEAR, 8 * i + 5),
        ))
        a_hop2.append((
            remote(a_send.at[top], a_second.at[top], NEAR, 8 * i + 6),
            remote(a_send.at[low], a_second.at[low], FAR, 8 * i + 7),
        ))

    def start(hop):
        for copy in hop:
            copy.start()

    def pick(chosen, other, pred):
        return lax.select(pred, chosen, other)

    def c_turn(i):
        top, low = spans(i)
        c_hop1[i][0].wait_recv()
        c_send[top] = pick(c_first[top], own_c[top], near_mine)
        c_hop2[i][0].start()
        c_hop1[i][1].wait_recv()
        c_send[low] = pick(c_first[low], own_c[low], far_other)
        c_hop2[i][1].start()

    def c_land(i):
        top, low = spans(i)
        c_hop2[i][0].wait_recv()
        cot[top] = pick(c_second[top], c_send[top], far_mine)
        c_hop2[i][1].wait_recv()
        cot[low] = pick(c_second[low], pick(c_first[low], own_c[low], far_mine), near_at_source)

    def a_turn(i):
        top, low = spans(i)
        a_hop1[i][0].wait_recv()
        a_send[top] = pick(a_first[top], att[top], far_mine)
        a_hop2[i][0].start()
        a_hop1[i][1].wait_recv()
        a_send[low] = pick(a_first[low], att[low], near_other)
        a_hop2[i][1].start()

    def a_store(i, which):
        span = spans(i)[which]
        return pltpu.make_async_copy(
            att_final.at[span], att_out.at[0, span], store_sem.at[3 + 2 * i + which]
        )

    def a_land(i):
        top, low = spans(i)
        a_hop2[i][0].wait_recv()
        att_final[top] = pick(a_second[top], a_send[top], near_mine)
        a_store(i, 0).start()
        a_hop2[i][1].wait_recv()
        att_final[low] = pick(a_second[low], pick(a_first[low], att[low], near_mine), far_at_source)
        a_store(i, 1).start()

    def sum_copies(s):
        return [
            pltpu.make_async_remote_copy(
                src_ref=part.at[s], dst_ref=sum_recv.at[s, j],
                send_sem=sum_send_sem.at[3 * s + j], recv_sem=sum_recv_sem.at[3 * s + j],
                device_id=peer(moves), device_id_type=MESH,
            )
            for j, moves in enumerate(stage_peers(stages[s]))
        ]

    def sum_start(s):
        for copy in sum_copies(s):
            copy.start()

    def sum_finish(s):
        for copy in sum_copies(s):
            copy.wait_recv()
        total = part[s] + sum_recv[s, 0]
        if len(stages[s]) == 2:
            total = total + (sum_recv[s, 1] + sum_recv[s, 2])
        if s + 1 < len(stages):
            part[s + 1] = total
            sum_start(s + 1)
        else:
            sum_out[...] = total

    total_rows = count_ref[0] + 4
    key_bias = jnp.where(
        lax.broadcasted_iota(jnp.int32, (1, length), 1) < total_rows, 0.0, -jnp.inf
    ).astype(F32)

    def columns(pair):
        return pl.ds(pl.multiple_of(pair * LANES, LANES), LANES)

    def halves(block):
        lane = lax.broadcasted_iota(jnp.int32, block.shape, 1)
        wide = block.astype(F32)
        return (
            jnp.where(lane < HEAD_DIM, wide, 0.0).astype(BF16),
            jnp.where(lane < HEAD_DIM, 0.0, wide).astype(BF16),
        )

    def row_valid():
        return lax.broadcasted_iota(jnp.int32, (length, LANES), 0) < total_rows

    def forward(pair, carry):
        cols = columns(pair)
        keys = k[:, cols]
        blend = None
        for j, (q_half, v_half) in enumerate(zip(halves(q[:, cols]), halves(v[:, cols]))):
            scores = nt_dot(q_half, keys) + key_bias
            top = jnp.max(scores, axis=1, keepdims=True)
            expd = jnp.exp2((scores - top) * EXP_SCALE)
            low = (expd * (1.0 / jnp.sum(expd, axis=1, keepdims=True))).astype(BF16)
            weights[2 * pair + j] = low
            term = nn_dot(low, v_half)
            blend = term if blend is None else blend + term
        mixed_low = blend.astype(BF16)
        mixed[:, cols] = mixed_low
        out = jnp.where(row_valid(), scale_ref[:, cols] * mixed_low.astype(F32), 0.0)
        att[:, cols] = out.astype(BF16)
        return carry

    def scale_part():
        part[0] = jnp.zeros((8, LANES), F32)
        for pair in range(pairs):
            cols = pl.ds(pair * LANES, LANES)
            product = cot[:, cols].astype(F32) * mixed[:, cols].astype(F32)
            part[0, pl.ds(pair, 1), :] = jnp.sum(
                jnp.where(row_valid(), product, 0.0), axis=0, keepdims=True
            )

    def backward(pair, carry):
        cols = columns(pair)
        up = jnp.where(row_valid(), cot[:, cols].astype(F32) * scale_ref[:, cols], 0.0)
        values = v[:, cols]
        blended = mixed[:, cols].astype(F32)
        dq_sum = dk_sum = dv_sum = None
        parts = zip(halves(up), halves(k[:, cols]), halves(q[:, cols]))
        for j, (up_half, k_half, q_half) in enumerate(parts):
            low = weights[2 * pair + j]
            delta = jnp.sum(up_half.astype(F32) * blended, axis=1, keepdims=True)
            grad = (low.astype(F32) * (nt_dot(up_half, values) - delta)).astype(BF16)
            dq_term, dk_term, dv_term = nn_dot(grad, k_half), tn_dot(grad, q_half), tn_dot(low, up_half)
            dq_sum = dq_term if j == 0 else dq_sum + dq_term
            dk_sum = dk_term if j == 0 else dk_sum + dk_term
            dv_sum = dv_term if j == 0 else dv_sum + dv_term
        dq[:, cols] = (dq_sum * FACTOR).astype(BF16)
        dk[:, cols] = (dk_sum * FACTOR).astype(BF16)
        dv[:, cols] = dv_sum.astype(BF16)
        return carry

    for i in range(PARTS):
        start(c_hop1[i])
    for copy in loads:
        copy.wait()
    lax.fori_loop(0, pairs // 2, forward, 0)
    c_turn(0)
    lax.fori_loop(pairs // 2, pairs, forward, 0)
    c_turn(1)
    c_turn(2)
    start(a_hop1[0])
    c_land(0)
    start(a_hop1[1])
    c_land(1)
    start(a_hop1[2])
    c_land(2)
    scale_part()
    sum_start(0)
    lax.fori_loop(0, pairs // 2, backward, 0)
    a_turn(0)
    sum_finish(0)
    lax.fori_loop(pairs // 2, pairs, backward, 0)
    grad_stores = [
        pltpu.make_async_copy(src, dst.at[0], store_sem.at[i])
        for i, (src, dst) in enumerate([(dq, dq_out), (dk, dk_out), (dv, dv_out)])
    ]
    for copy in grad_stores:
        copy.start()
    sum_finish(1)
    a_turn(1)
    sum_finish(2)
    a_turn(2)
    for s in range(3, len(stages)):
        sum_finish(s)
    for i in range(PARTS):
        a_land(i)
    for copy in grad_stores:
        copy.wait()
    for i in range(PARTS):
        for hop in (c_hop1[i], c_hop2[i], a_hop1[i], a_hop2[i]):
            for copy in hop:
                copy.wait_send()
        a_store(i, 0).wait()
        a_store(i, 1).wait()
    for s in range(len(stages)):
        for copy in sum_copies(s):
            copy.wait_send()


def per_device(stages, query_rows, key_rows, value_rows, cotangent, kept_counts, trades, layer_scale):
    _, length, width = query_rows.shape
    heads = width // HEAD_DIM
    image = jax.ShapeDtypeStruct(query_rows.shape, BF16)
    block = pltpu.VMEM((length, width), BF16)
    hbm = pl.BlockSpec(memory_space=pl.ANY)
    smem = pl.BlockSpec(memory_space=pltpu.SMEM)
    vmem = pl.BlockSpec(memory_space=pltpu.VMEM)
    slots = 8 * PARTS
    attended, query_grad, key_grad, value_grad, scale_sum = pl.pallas_call(
        functools.partial(kernel, stages),
        out_shape=(image, image, image, image, jax.ShapeDtypeStruct((8, LANES), F32)),
        in_specs=[hbm, hbm, hbm, hbm, smem, smem, vmem],
        out_specs=(hbm, hbm, hbm, hbm, vmem),
        scratch_shapes=[
            *[block] * 13,
            pltpu.VMEM((heads, length, length), BF16),
            *[block] * 4,
            pltpu.VMEM((len(stages), 8, LANES), F32),
            pltpu.VMEM((len(stages), 3, 8, LANES), F32),
            pltpu.SemaphoreType.DMA((4,)),
            pltpu.SemaphoreType.DMA((3 + 2 * PARTS,)),
            pltpu.SemaphoreType.DMA((slots,)),
            pltpu.SemaphoreType.DMA((slots,)),
            pltpu.SemaphoreType.DMA((3 * len(stages),)),
            pltpu.SemaphoreType.DMA((3 * len(stages),)),
        ],
        compiler_params=pltpu.CompilerParams(
            collective_id=0, has_side_effects=True, vmem_limit_bytes=60 * 2**20
        ),
        cost_estimate=pl.CostEstimate(
            flops=12 * heads * length * length * HEAD_DIM,
            bytes_accessed=16 * length * width,
            transcendentals=heads * length * length,
        ),
    )(
        query_rows, key_rows, value_rows, cotangent,
        kept_counts, trades.T, layer_scale.reshape(1, width),
    )
    scale_grad = scale_sum[: width // LANES].reshape(width)
    return attended, query_grad, key_grad, value_grad, scale_grad


def solution(mesh):
    rows = P(("dp", "group"), None, None)
    return jax.shard_map(
        functools.partial(per_device, sum_stages(mesh.shape["dp"])),
        mesh=mesh,
        in_specs=(rows, rows, rows, rows, P(("dp", "group")), P(), P()),
        out_specs=(rows, rows, rows, rows, P()),
        check_vma=False,
    )
```

```python
import functools
import math

import jax
import jax.numpy as jnp
from jax import lax
from jax.experimental import pallas as pl
from jax.experimental.pallas import tpu as pltpu
from jax.sharding import PartitionSpec as P

MESH = pl.DeviceIdType.MESH
BF16 = jnp.bfloat16
F32 = jnp.float32
HEAD_DIM = 64
LANES = 128
FACTOR = HEAD_DIM ** -0.5
EXP_SCALE = FACTOR * math.log2(math.e)
PARTS = 3

NEAR, FAR = 4, 8


def flip(index, bit):
    return index + bit * (1 - 2 * ((index // bit) % 2))


def nt_dot(a, b):
    return lax.dot_general(a, b, (((1,), (1,)), ((), ())), preferred_element_type=F32)


def tn_dot(a, b):
    return lax.dot_general(a, b, (((0,), (0,)), ((), ())), preferred_element_type=F32)


def nn_dot(a, b):
    return jnp.dot(a, b, preferred_element_type=F32)


def sum_stages(dp_size):
    top = dp_size // 2
    middle, bit = [], 2
    while bit < top:
        middle.insert(0, ("dp", bit))
        bit *= 2
    stages = [
        [("group", 2), ("group", 1), ("dp", 1)], middle, [("dp", top), ("group", FAR), ("group", NEAR)]
    ]
    return [stage for stage in stages if stage]


def stage_moves(stage):
    count = len(stage)
    return [
        [stage[i] for i in range(count) if choice >> (count - 1 - i) & 1]
        for choice in range(1, 2**count)
    ]


def kernel(
    stages,
    q_hbm, k_hbm, v_hbm, c_hbm, count_hbm, trades_hbm, scale_hbm,
    att_final, dq, dk, dv, sum_out,
    q, k, v, own_c, c_first, c_send, c_second, cot,
    att, a_first, a_send, a_second,
    weights, mixed, part, sum_recv, scale_ref, count_ref, trades_ref,
    load_sem, send_sem, recv_sem, sum_send_sem, sum_recv_sem, ready,
):
    g = lax.axis_index("group")
    d = lax.axis_index("dp")
    length, width = q.shape
    pairs = width // LANES
    half = length // 2
    rows = half // PARTS

    def peer(moves):
        pg, pd = g, d
        for axis, bit in moves:
            if axis == "group":
                pg = flip(pg, bit)
            else:
                pd = flip(pd, bit)
        return (pd, pg)

    def upper(moves):
        axis, bit = moves[0]
        return ((g if axis == "group" else d) // bit) % 2

    loads = [
        pltpu.make_async_copy(src, dst, load_sem.at[i])
        for i, (src, dst) in enumerate([
            (q_hbm.at[0], q), (k_hbm.at[0], k), (v_hbm.at[0], v), (c_hbm.at[0], own_c),
            (count_hbm, count_ref), (trades_hbm, trades_ref), (scale_hbm, scale_ref),
        ])
    ]
    for copy in loads:
        copy.start()

    meetings = [moves for stage in stages for moves in stage_moves(stage)]
    barrier = pltpu.get_barrier_semaphore()
    greetings = 0
    for moves in meetings:
        greetings = greetings + upper(moves)

        @pl.when(upper(moves) == 0)
        def _(moves=moves):
            pl.semaphore_signal(barrier, inc=1, device_id=peer(moves), device_id_type=MESH)

    @pl.when(greetings > 0)
    def _():
        pl.semaphore_wait(barrier, greetings)

    for j, moves in enumerate(meetings):

        @pl.when(upper(moves) == 1)
        def _(j=j, moves=moves):
            pl.semaphore_signal(ready.at[j], inc=1, device_id=peer(moves), device_id_type=MESH)

    met = []

    def meet(moves):
        j = meetings.index(moves)
        if j in met:
            return
        met.append(j)

        @pl.when(upper(moves) == 0)
        def _():
            pl.semaphore_wait(ready.at[j], 1)

    def spans(part_index):
        return pl.ds(part_index * rows, rows), pl.ds(half + part_index * rows, rows)

    def remote(src, dst, bit, slot):
        return pltpu.make_async_remote_copy(
            src_ref=src, dst_ref=dst, send_sem=send_sem.at[slot], recv_sem=recv_sem.at[slot],
            device_id=peer([("group", bit)]), device_id_type=MESH,
        )

    c_hop1, c_hop2, a_hop1, a_hop2 = [], [], [], []
    for i in range(PARTS):
        top, low = spans(i)
        c_hop1.append((
            remote(c_hbm.at[0, top], c_first.at[top], NEAR, 8 * i),
            remote(c_hbm.at[0, low], c_first.at[low], FAR, 8 * i + 1),
        ))
        c_hop2.append((
            remote(c_send.at[top], c_second.at[top], FAR, 8 * i + 2),
            remote(c_send.at[low], c_second.at[low], NEAR, 8 * i + 3),
        ))
        a_hop1.append((
            remote(att.at[top], a_first.at[top], FAR, 8 * i + 4),
            remote(att.at[low], a_first.at[low], NEAR, 8 * i + 5),
        ))
        a_hop2.append((
            remote(a_send.at[top], a_second.at[top], NEAR, 8 * i + 6),
            remote(a_send.at[low], a_second.at[low], FAR, 8 * i + 7),
        ))

    def start(hop):
        for copy in hop:
            copy.start()

    def pick(chosen, other, pred):
        return lax.select(pred, chosen, other)

    def c_turn(i):
        top, low = spans(i)
        c_hop1[i][0].wait_recv()
        c_send[top] = pick(c_first[top], own_c[top], near_mine)
        c_hop2[i][0].start()
        c_hop1[i][1].wait_recv()
        c_send[low] = pick(c_first[low], own_c[low], far_other)
        c_hop2[i][1].start()

    def c_land(i):
        top, low = spans(i)
        c_hop2[i][0].wait_recv()
        cot[top] = pick(c_second[top], c_send[top], far_mine)
        c_hop2[i][1].wait_recv()
        cot[low] = pick(c_second[low], pick(c_first[low], own_c[low], far_mine), near_at_source)

    def a_turn(i):
        top, low = spans(i)
        a_hop1[i][0].wait_recv()
        a_send[top] = pick(a_first[top], att[top], far_mine)
        a_hop2[i][0].start()
        a_hop1[i][1].wait_recv()
        a_send[low] = pick(a_first[low], att[low], near_other)
        a_hop2[i][1].start()

    def a_land(i):
        top, low = spans(i)
        a_hop2[i][0].wait_recv()
        att_final[0, top] = pick(a_second[top], a_send[top], near_mine)
        a_hop2[i][1].wait_recv()
        att_final[0, low] = pick(a_second[low], pick(a_first[low], att[low], near_mine), far_at_source)

    def sum_copies(s):
        return [
            pltpu.make_async_remote_copy(
                src_ref=part.at[s], dst_ref=sum_recv.at[s, j],
                send_sem=sum_send_sem.at[7 * s + j], recv_sem=sum_recv_sem.at[7 * s + j],
                device_id=peer(moves), device_id_type=MESH,
            )
            for j, moves in enumerate(stage_moves(stages[s]))
        ]

    def sum_start(s):
        for moves in stage_moves(stages[s]):
            meet(moves)
        for copy in sum_copies(s):
            copy.start()

    def sum_finish(s):
        for copy in sum_copies(s):
            copy.wait_recv()
        terms = [part[s]] + [sum_recv[s, j] for j in range(len(stage_moves(stages[s])))]
        while len(terms) > 1:
            terms = [terms[i] + terms[i + 1] for i in range(0, len(terms), 2)]
        if s + 1 < len(stages):
            part[s + 1] = terms[0]
            sum_start(s + 1)
        else:
            sum_out[...] = terms[0][: width // LANES]

    start_near = [c_hop1[i][0] for i in range(PARTS)]
    start_far = [c_hop1[i][1] for i in range(PARTS)]
    meet([("group", NEAR)])
    start(start_near)
    meet([("group", FAR)])
    start(start_far)
    for copy in loads:
        copy.wait()

    a, b, x = g // 8, (g // 4) % 2, g % 4
    base = d * 16 + x

    def flag(offset, round_index):
        return trades_ref[round_index, base + offset] == 1

    far_mine, far_other = flag(b * 4, 0), flag((1 - b) * 4, 0)
    near_mine, near_other = flag(a * 8, 1), flag((1 - a) * 8, 1)
    near_at_source = jnp.logical_or(
        jnp.logical_and(far_mine, near_other),
        jnp.logical_and(jnp.logical_not(far_mine), near_mine),
    )
    far_at_source = jnp.logical_or(
        jnp.logical_and(near_mine, far_other),
        jnp.logical_and(jnp.logical_not(near_mine), far_mine),
    )

    total_rows = count_ref[0] + 4
    key_bias = jnp.where(
        lax.broadcasted_iota(jnp.int32, (1, length), 1) < total_rows, 0.0, -jnp.inf
    ).astype(F32)

    def columns(pair):
        return pl.ds(pl.multiple_of(pair * LANES, LANES), LANES)

    def halves(block):
        lane = lax.broadcasted_iota(jnp.int32, block.shape, 1)
        wide = block.astype(F32)
        return (
            jnp.where(lane < HEAD_DIM, wide, 0.0).astype(BF16),
            jnp.where(lane < HEAD_DIM, 0.0, wide).astype(BF16),
        )

    def row_valid():
        return lax.broadcasted_iota(jnp.int32, (length, LANES), 0) < total_rows

    def forward(pair, carry):
        cols = columns(pair)
        keys = k[:, cols]
        blend = None
        for j, (q_half, v_half) in enumerate(zip(halves(q[:, cols]), halves(v[:, cols]))):
            scores = nt_dot(q_half, keys) + key_bias
            top = jnp.max(scores, axis=1, keepdims=True)
            expd = jnp.exp2((scores - top) * EXP_SCALE)
            low = (expd * (1.0 / jnp.sum(expd, axis=1, keepdims=True))).astype(BF16)
            weights[2 * pair + j] = low
            term = nn_dot(low, v_half)
            blend = term if blend is None else blend + term
        mixed_low = blend.astype(BF16)
        mixed[:, cols] = mixed_low
        out = jnp.where(row_valid(), scale_ref[pl.ds(pair, 1), :] * mixed_low.astype(F32), 0.0)
        att[:, cols] = out.astype(BF16)
        return carry

    def scale_part():
        part[0] = jnp.zeros((8, LANES), F32)
        for pair in range(pairs):
            cols = pl.ds(pair * LANES, LANES)
            product = cot[:, cols].astype(F32) * mixed[:, cols].astype(F32)
            part[0, pl.ds(pair, 1), :] = jnp.sum(
                jnp.where(row_valid(), product, 0.0), axis=0, keepdims=True
            )

    def backward(pair, carry):
        cols = columns(pair)
        up = jnp.where(row_valid(), cot[:, cols].astype(F32) * scale_ref[pl.ds(pair, 1), :], 0.0)
        values = v[:, cols]
        blended = mixed[:, cols].astype(F32)
        dq_sum = dk_sum = dv_sum = None
        parts = zip(halves(up), halves(k[:, cols]), halves(q[:, cols]))
        for j, (up_half, k_half, q_half) in enumerate(parts):
            low = weights[2 * pair + j]
            delta = jnp.sum(up_half.astype(F32) * blended, axis=1, keepdims=True)
            grad = (low.astype(F32) * (nt_dot(up_half, values) - delta)).astype(BF16)
            dq_term, dk_term, dv_term = nn_dot(grad, k_half), tn_dot(grad, q_half), tn_dot(low, up_half)
            dq_sum = dq_term if j == 0 else dq_sum + dq_term
            dk_sum = dk_term if j == 0 else dk_sum + dk_term
            dv_sum = dv_term if j == 0 else dv_sum + dv_term
        dq[0, :, cols] = (dq_sum * FACTOR).astype(BF16)
        dk[0, :, cols] = (dk_sum * FACTOR).astype(BF16)
        dv[0, :, cols] = dv_sum.astype(BF16)
        return carry

    lax.fori_loop(0, pairs // 2, forward, 0)
    c_turn(0)
    lax.fori_loop(pairs // 2, pairs, forward, 0)
    c_turn(1)
    c_turn(2)
    start(a_hop1[0])
    c_land(0)
    start(a_hop1[1])
    c_land(1)
    start(a_hop1[2])
    c_land(2)
    scale_part()
    sum_start(0)
    lax.fori_loop(0, 3, backward, 0)
    sum_finish(0)
    a_turn(0)
    lax.fori_loop(3, pairs, backward, 0)
    for s in range(1, len(stages) - 1):
        sum_finish(s)
    a_turn(1)
    a_turn(2)
    sum_finish(len(stages) - 1)
    for i in range(PARTS):
        a_land(i)
    for i in range(PARTS):
        for hop in (c_hop1[i], c_hop2[i], a_hop1[i], a_hop2[i]):
            for copy in hop:
                copy.wait_send()
    for s in range(len(stages)):
        for copy in sum_copies(s):
            copy.wait_send()


def settle(*refs):
    half = len(refs) // 2
    sources, results, sem = refs[:half], refs[half:-1], refs[-1]
    copies = [
        pltpu.make_async_copy(src, dst, sem.at[i])
        for i, (src, dst) in enumerate(zip(sources, results))
    ]
    for copy in copies:
        copy.start()
    for copy in copies:
        copy.wait()


def per_device(stages, query_rows, key_rows, value_rows, cotangent, kept_counts, trades, layer_scale):
    _, length, width = query_rows.shape
    heads = width // HEAD_DIM
    tiles = width // LANES
    block = pltpu.VMEM((length, width), BF16)
    image = pltpu.VMEM((1, length, width), BF16)
    hbm = pl.BlockSpec(memory_space=pl.ANY)
    vmem = pl.BlockSpec(memory_space=pltpu.VMEM)
    slots = 8 * PARTS
    meetings = sum(len(stage_moves(stage)) for stage in stages)
    results = pl.pallas_call(
        functools.partial(kernel, stages),
        out_shape=(image, image, image, image, pltpu.VMEM((tiles, LANES), F32)),
        in_specs=[hbm] * 7,
        out_specs=(vmem,) * 5,
        scratch_shapes=[
            *[block] * 12,
            pltpu.VMEM((heads, length, length), BF16),
            block,
            pltpu.VMEM((len(stages), 8, LANES), F32),
            pltpu.VMEM((len(stages), 7, 8, LANES), F32),
            pltpu.VMEM((tiles, LANES), F32),
            pltpu.SMEM((1,), jnp.int32),
            pltpu.SMEM(trades.shape[::-1], jnp.int32),
            pltpu.SemaphoreType.DMA((7,)),
            pltpu.SemaphoreType.DMA((slots,)),
            pltpu.SemaphoreType.DMA((slots,)),
            pltpu.SemaphoreType.DMA((7 * len(stages),)),
            pltpu.SemaphoreType.DMA((7 * len(stages),)),
            pltpu.SemaphoreType.REGULAR((meetings,)),
        ],
        compiler_params=pltpu.CompilerParams(
            collective_id=0, has_side_effects=True, vmem_limit_bytes=52 * 2**20
        ),
        cost_estimate=pl.CostEstimate(
            flops=12 * heads * length * length * HEAD_DIM,
            bytes_accessed=16 * length * width,
            transcendentals=heads * length * length,
        ),
    )(
        query_rows, key_rows, value_rows, cotangent,
        kept_counts, trades.T, layer_scale.reshape(tiles, LANES),
    )
    attended, query_grad, key_grad, value_grad, scale_sum = pl.pallas_call(
        settle,
        out_shape=tuple(jax.ShapeDtypeStruct(item.shape, item.dtype) for item in results),
        in_specs=[hbm] * 5,
        out_specs=(hbm,) * 5,
        scratch_shapes=[pltpu.SemaphoreType.DMA((5,))],
        compiler_params=pltpu.CompilerParams(vmem_limit_bytes=2**20),
    )(*results)
    return attended, query_grad, key_grad, value_grad, scale_sum.reshape(width)


def solution(mesh):
    rows = P(("dp", "group"), None, None)
    return jax.shard_map(
        functools.partial(per_device, sum_stages(mesh.shape["dp"])),
        mesh=mesh,
        in_specs=(rows, rows, rows, rows, P(("dp", "group")), P(), P()),
        out_specs=(rows, rows, rows, rows, P()),
        check_vma=False,
    )
```

```python
import functools
import math

import jax
import jax.numpy as jnp
from jax import lax
from jax.experimental import pallas as pl
from jax.experimental.pallas import tpu as pltpu
from jax.sharding import PartitionSpec as P

MESH = pl.DeviceIdType.MESH
BF16 = jnp.bfloat16
F32 = jnp.float32
HEAD_DIM = 64
LANES = 128
FACTOR = HEAD_DIM ** -0.5
EXP_SCALE = FACTOR * math.log2(math.e)
PARTS = 4

NEAR, FAR = 4, 8


def flip(index, bit):
    return index + bit * (1 - 2 * ((index // bit) % 2))


def nt_dot(a, b):
    return lax.dot_general(a, b, (((1,), (1,)), ((), ())), preferred_element_type=F32)


def tn_dot(a, b):
    return lax.dot_general(a, b, (((0,), (0,)), ((), ())), preferred_element_type=F32)


def nn_dot(a, b):
    return jnp.dot(a, b, preferred_element_type=F32)


def sum_stages(dp_size):
    top = dp_size // 2
    middle, bit = [], 2
    while bit < top:
        middle.insert(0, ("dp", bit))
        bit *= 2
    stages = [
        [("dp", top), ("group", FAR), ("group", NEAR)], [("group", 2), ("group", 1), ("dp", 1)], middle
    ]
    return [stage for stage in stages if stage]


def stage_moves(stage):
    count = len(stage)
    return [
        [stage[i] for i in range(count) if choice >> (count - 1 - i) & 1]
        for choice in range(1, 2**count)
    ]


def kernel(
    stages,
    q_hbm, k_hbm, v_hbm, c_hbm, count_hbm, trades_hbm, scale_hbm,
    att_final, dq, dk, dv, sum_out,
    q, k, v, own_c, c_first, c_send, c_second, cot,
    att, a_first, a_send, a_second,
    weights, mixed, part, sum_recv, scale_ref, count_ref, trades_ref,
    load_sem, send_sem, recv_sem, sum_send_sem, sum_recv_sem, ready,
):
    g = lax.axis_index("group")
    d = lax.axis_index("dp")
    length, width = q.shape
    pairs = width // LANES
    half = length // 2
    rows = half // PARTS

    def peer(moves):
        pg, pd = g, d
        for axis, bit in moves:
            if axis == "group":
                pg = flip(pg, bit)
            else:
                pd = flip(pd, bit)
        return (pd, pg)

    def rank(pd, pg):
        size = 2 ** sum(axis == "dp" for stage in stages for axis, _ in stage)
        ny = size // 4
        z, x = pd // (size // 2) * 4 + pg // 4, pg % 4
        y, core = (pd // 2) % ny, pd % 2
        y = jnp.where(2 * y < ny, y, ny // 2 + ny - 1 - y)
        place = 2 * (((z * ny + y) * 4 + x) * 2 + 1 - core)
        return jnp.where(pd + pg == 0, 64 * ny - 1, place)

    def upper(moves):
        return rank(d, g) > rank(*peer(moves))

    loads = [
        pltpu.make_async_copy(src, dst, load_sem.at[i])
        for i, (src, dst) in enumerate([
            (q_hbm.at[0], q), (k_hbm.at[0], k), (v_hbm.at[0], v), (c_hbm.at[0], own_c),
            (count_hbm, count_ref), (trades_hbm, trades_ref), (scale_hbm, scale_ref),
        ])
    ]

    meetings = [moves for stage in stages for moves in stage_moves(stage)]
    meetings.sort(key=lambda moves: moves not in ([("group", NEAR)], [("group", FAR)]))
    barrier = pltpu.get_barrier_semaphore()
    greetings = 0
    for moves in meetings:
        greetings = greetings + upper(moves).astype(jnp.int32)

        @pl.when(jnp.logical_not(upper(moves)))
        def _(moves=moves):
            pl.semaphore_signal(barrier, inc=1, device_id=peer(moves), device_id_type=MESH)

    @pl.when(greetings > 0)
    def _():
        pl.semaphore_wait(barrier, greetings)

    for j, moves in enumerate(meetings):

        @pl.when(upper(moves))
        def _(j=j, moves=moves):
            pl.semaphore_signal(ready.at[j], inc=1, device_id=peer(moves), device_id_type=MESH)

    met = []

    def meet(moves):
        j = meetings.index(moves)
        if j in met:
            return
        met.append(j)

        @pl.when(jnp.logical_not(upper(moves)))
        def _():
            pl.semaphore_wait(ready.at[j], 1)

    def spans(part_index):
        return pl.ds(part_index * rows, rows), pl.ds(half + part_index * rows, rows)

    def remote(src, dst, bit, slot):
        return pltpu.make_async_remote_copy(
            src_ref=src, dst_ref=dst, send_sem=send_sem.at[slot], recv_sem=recv_sem.at[slot],
            device_id=peer([("group", bit)]), device_id_type=MESH,
        )

    c_hop1, c_hop2, a_hop1, a_hop2 = [], [], [], []
    for i in range(PARTS):
        top, low = spans(i)
        c_hop1.append((
            remote(c_hbm.at[0, top], c_first.at[top], NEAR, 8 * i),
            remote(c_hbm.at[0, low], c_first.at[low], FAR, 8 * i + 1),
        ))
        c_hop2.append((
            remote(c_send.at[top], c_second.at[top], FAR, 8 * i + 2),
            remote(c_send.at[low], c_second.at[low], NEAR, 8 * i + 3),
        ))
        a_hop1.append((
            remote(att.at[top], a_first.at[top], FAR, 8 * i + 4),
            remote(att.at[low], a_first.at[low], NEAR, 8 * i + 5),
        ))
        a_hop2.append((
            remote(a_send.at[top], a_second.at[top], NEAR, 8 * i + 6),
            remote(a_send.at[low], a_second.at[low], FAR, 8 * i + 7),
        ))

    def start(hop):
        for copy in hop:
            copy.start()

    def pick(chosen, other, pred):
        return lax.select(pred, chosen, other)

    def c_turn(i):
        top, low = spans(i)
        c_hop1[i][0].wait_recv()
        c_send[top] = pick(c_first[top], own_c[top], near_mine)
        c_hop2[i][0].start()
        c_hop1[i][1].wait_recv()
        c_send[low] = pick(c_first[low], own_c[low], far_other)
        c_hop2[i][1].start()

    def c_land(i):
        top, low = spans(i)
        c_hop2[i][0].wait_recv()
        cot[top] = pick(c_second[top], c_send[top], far_mine)
        c_hop2[i][1].wait_recv()
        cot[low] = pick(c_second[low], pick(c_first[low], own_c[low], far_mine), near_at_source)

    def a_turn(i):
        top, low = spans(i)
        a_hop1[i][0].wait_recv()
        a_send[top] = pick(a_first[top], att[top], far_mine)
        a_hop2[i][0].start()
        a_hop1[i][1].wait_recv()
        a_send[low] = pick(a_first[low], att[low], near_other)
        a_hop2[i][1].start()

    def a_land(i):
        top, low = spans(i)
        a_hop2[i][0].wait_recv()
        att_final[0, top] = pick(a_second[top], a_send[top], near_mine)
        a_hop2[i][1].wait_recv()
        att_final[0, low] = pick(a_second[low], pick(a_first[low], att[low], near_mine), far_at_source)

    def sum_copies(s):
        return [
            pltpu.make_async_remote_copy(
                src_ref=part.at[s], dst_ref=sum_recv.at[s, j],
                send_sem=sum_send_sem.at[7 * s + j], recv_sem=sum_recv_sem.at[7 * s + j],
                device_id=peer(moves), device_id_type=MESH,
            )
            for j, moves in enumerate(stage_moves(stages[s]))
        ]

    def sum_start(s):
        for moves in stage_moves(stages[s]):
            meet(moves)
        for copy in sum_copies(s):
            copy.start()

    def sum_finish(s):
        for copy in sum_copies(s):
            copy.wait_recv()
        terms = [part[s]] + [sum_recv[s, j] for j in range(len(stage_moves(stages[s])))]
        while len(terms) > 1:
            terms = [terms[i] + terms[i + 1] for i in range(0, len(terms), 2)]
        if s + 1 < len(stages):
            part[s + 1] = terms[0]
            sum_start(s + 1)
        else:
            sum_out[...] = terms[0][: width // LANES]

    meet([("group", NEAR)])
    c_hop1[0][0].start()
    meet([("group", FAR)])
    c_hop1[0][1].start()
    for i in range(1, PARTS):
        start(c_hop1[i])
    for copy in loads:
        copy.start()
    for copy in loads:
        copy.wait()

    a, b, x = g // 8, (g // 4) % 2, g % 4
    base = d * 16 + x

    def flag(offset, round_index):
        return trades_ref[round_index, base + offset] == 1

    far_mine, far_other = flag(b * 4, 0), flag((1 - b) * 4, 0)
    near_mine, near_other = flag(a * 8, 1), flag((1 - a) * 8, 1)
    near_at_source = jnp.logical_or(
        jnp.logical_and(far_mine, near_other),
        jnp.logical_and(jnp.logical_not(far_mine), near_mine),
    )
    far_at_source = jnp.logical_or(
        jnp.logical_and(near_mine, far_other),
        jnp.logical_and(jnp.logical_not(near_mine), far_mine),
    )

    total_rows = count_ref[0] + 4
    key_bias = jnp.where(
        lax.broadcasted_iota(jnp.int32, (1, length), 1) < total_rows, 0.0, -jnp.inf
    ).astype(F32)

    def columns(pair):
        return pl.ds(pl.multiple_of(pair * LANES, LANES), LANES)

    def halves(block):
        lane = lax.broadcasted_iota(jnp.int32, block.shape, 1)
        wide = block.astype(F32)
        return (
            jnp.where(lane < HEAD_DIM, wide, 0.0).astype(BF16),
            jnp.where(lane < HEAD_DIM, 0.0, wide).astype(BF16),
        )

    def row_valid():
        return lax.broadcasted_iota(jnp.int32, (length, LANES), 0) < total_rows

    def forward(pair, carry):
        cols = columns(pair)
        keys = k[:, cols]
        blend = None
        for j, (q_half, v_half) in enumerate(zip(halves(q[:, cols]), halves(v[:, cols]))):
            scores = nt_dot(q_half, keys) + key_bias
            top = jnp.max(scores, axis=1, keepdims=True)
            expd = jnp.exp2((scores - top) * EXP_SCALE)
            low = (expd * (1.0 / jnp.sum(expd, axis=1, keepdims=True))).astype(BF16)
            weights[2 * pair + j] = low
            term = nn_dot(low, v_half)
            blend = term if blend is None else blend + term
        mixed_low = blend.astype(BF16)
        mixed[:, cols] = mixed_low
        out = jnp.where(row_valid(), scale_ref[pl.ds(pair, 1), :] * mixed_low.astype(F32), 0.0)
        att[:, cols] = out.astype(BF16)
        return carry

    def scale_rows(begin):
        valid = begin + lax.broadcasted_iota(jnp.int32, (rows, LANES), 0) < total_rows
        for pair in range(pairs):
            cols = pl.ds(pair * LANES, LANES)
            span = pl.ds(begin, rows)
            product = cot[span, cols].astype(F32) * mixed[span, cols].astype(F32)
            part[0, pl.ds(pair, 1), :] += jnp.sum(
                jnp.where(valid, product, 0.0), axis=0, keepdims=True
            )

    def backward(pair, carry):
        cols = columns(pair)
        up = jnp.where(row_valid(), cot[:, cols].astype(F32) * scale_ref[pl.ds(pair, 1), :], 0.0)
        values = v[:, cols]
        blended = mixed[:, cols].astype(F32)
        dq_sum = dk_sum = dv_sum = None
        parts = zip(halves(up), halves(k[:, cols]), halves(q[:, cols]))
        for j, (up_half, k_half, q_half) in enumerate(parts):
            low = weights[2 * pair + j]
            delta = jnp.sum(up_half.astype(F32) * blended, axis=1, keepdims=True)
            grad = (low.astype(F32) * (nt_dot(up_half, values) - delta)).astype(BF16)
            dq_term, dk_term, dv_term = nn_dot(grad, k_half), tn_dot(grad, q_half), tn_dot(low, up_half)
            dq_sum = dq_term if j == 0 else dq_sum + dq_term
            dk_sum = dk_term if j == 0 else dk_sum + dk_term
            dv_sum = dv_term if j == 0 else dv_sum + dv_term
        dq[0, :, cols] = (dq_sum * FACTOR).astype(BF16)
        dk[0, :, cols] = (dk_sum * FACTOR).astype(BF16)
        dv[0, :, cols] = dv_sum.astype(BF16)
        return carry

    lax.fori_loop(0, pairs // 2, forward, 0)
    c_turn(0)
    lax.fori_loop(pairs // 2, pairs, forward, 0)
    for i in range(1, PARTS):
        c_turn(i)
    start(a_hop1[0])
    part[0] = jnp.zeros((8, LANES), F32)
    for i in range(PARTS):
        c_land(i)
        scale_rows(i * rows)
        scale_rows(half + i * rows)
    sum_start(0)
    for i in range(1, PARTS):
        start(a_hop1[i])
    lax.fori_loop(0, pairs // 2, backward, 0)
    a_turn(0)
    lax.fori_loop(pairs // 2, pairs, backward, 0)
    for i in range(1, PARTS):
        a_turn(i)
    for s in range(len(stages) - 1):
        sum_finish(s)
    for i in range(PARTS - 1):
        a_land(i)
    sum_finish(len(stages) - 1)
    a_land(PARTS - 1)
    for i in range(PARTS):
        for hop in (c_hop1[i], c_hop2[i], a_hop1[i], a_hop2[i]):
            for copy in hop:
                copy.wait_send()
    for s in range(len(stages)):
        for copy in sum_copies(s):
            copy.wait_send()


def settle(*refs):
    half = len(refs) // 2
    sources, results, sem = refs[:half], refs[half:-1], refs[-1]
    copies = [
        pltpu.make_async_copy(src, dst, sem.at[i])
        for i, (src, dst) in enumerate(zip(sources, results))
    ]
    for copy in copies:
        copy.start()
    for copy in copies:
        copy.wait()


def per_device(stages, query_rows, key_rows, value_rows, cotangent, kept_counts, trades, layer_scale):
    _, length, width = query_rows.shape
    heads = width // HEAD_DIM
    tiles = width // LANES
    block = pltpu.VMEM((length, width), BF16)
    image = pltpu.VMEM((1, length, width), BF16)
    hbm = pl.BlockSpec(memory_space=pl.ANY)
    vmem = pl.BlockSpec(memory_space=pltpu.VMEM)
    slots = 8 * PARTS
    meetings = sum(len(stage_moves(stage)) for stage in stages)
    results = pl.pallas_call(
        functools.partial(kernel, stages),
        out_shape=(image, image, image, image, pltpu.VMEM((tiles, LANES), F32)),
        in_specs=[hbm] * 7,
        out_specs=(vmem,) * 5,
        scratch_shapes=[
            *[block] * 12,
            pltpu.VMEM((heads, length, length), BF16),
            block,
            pltpu.VMEM((len(stages), 8, LANES), F32),
            pltpu.VMEM((len(stages), 7, 8, LANES), F32),
            pltpu.VMEM((tiles, LANES), F32),
            pltpu.SMEM((1,), jnp.int32),
            pltpu.SMEM(trades.shape[::-1], jnp.int32),
            pltpu.SemaphoreType.DMA((7,)),
            pltpu.SemaphoreType.DMA((slots,)),
            pltpu.SemaphoreType.DMA((slots,)),
            pltpu.SemaphoreType.DMA((7 * len(stages),)),
            pltpu.SemaphoreType.DMA((7 * len(stages),)),
            pltpu.SemaphoreType.REGULAR((meetings,)),
        ],
        compiler_params=pltpu.CompilerParams(
            collective_id=0, has_side_effects=True, vmem_limit_bytes=52 * 2**20
        ),
        cost_estimate=pl.CostEstimate(
            flops=12 * heads * length * length * HEAD_DIM,
            bytes_accessed=16 * length * width,
            transcendentals=heads * length * length,
        ),
    )(
        query_rows, key_rows, value_rows, cotangent,
        kept_counts, trades.T, layer_scale.reshape(tiles, LANES),
    )
    attended, query_grad, key_grad, value_grad, scale_sum = pl.pallas_call(
        settle,
        out_shape=tuple(jax.ShapeDtypeStruct(item.shape, item.dtype) for item in results),
        in_specs=[hbm] * 5,
        out_specs=(hbm,) * 5,
        scratch_shapes=[pltpu.SemaphoreType.DMA((5,))],
        compiler_params=pltpu.CompilerParams(vmem_limit_bytes=2**20),
    )(*results)
    return attended, query_grad, key_grad, value_grad, scale_sum.reshape(width)


def solution(mesh):
    rows = P(("dp", "group"), None, None)
    return jax.shard_map(
        functools.partial(per_device, sum_stages(mesh.shape["dp"])),
        mesh=mesh,
        in_specs=(rows, rows, rows, rows, P(("dp", "group")), P(), P()),
        out_specs=(rows, rows, rows, rows, P()),
        check_vma=False,
    )
```

```python
import functools
import math

import jax
import jax.numpy as jnp
from jax import lax
from jax.experimental import pallas as pl
from jax.experimental.pallas import tpu as pltpu
from jax.sharding import PartitionSpec as P

MESH = pl.DeviceIdType.MESH
BF16 = jnp.bfloat16
F32 = jnp.float32
HEAD_DIM = 64
LANES = 128
FACTOR = HEAD_DIM ** -0.5
EXP_SCALE = FACTOR * math.log2(math.e)
PARTS = 4

NEAR, FAR = 4, 8


def flip(index, bit):
    return index + bit * (1 - 2 * ((index // bit) % 2))


def nt_dot(a, b):
    return lax.dot_general(a, b, (((1,), (1,)), ((), ())), preferred_element_type=F32)


def tn_dot(a, b):
    return lax.dot_general(a, b, (((0,), (0,)), ((), ())), preferred_element_type=F32)


def nn_dot(a, b):
    return jnp.dot(a, b, preferred_element_type=F32)


def sum_stages(dp_size):
    top = dp_size // 2
    middle, bit = [], 2
    while bit < top:
        middle.insert(0, ("dp", bit))
        bit *= 2
    stages = [
        [("dp", top), ("group", FAR), ("group", NEAR)], [("group", 2), ("group", 1), ("dp", 1)], middle
    ]
    return [stage for stage in stages if stage]


def stage_moves(stage):
    count = len(stage)
    return [
        [stage[i] for i in range(count) if choice >> (count - 1 - i) & 1]
        for choice in range(1, 2**count)
    ]


def kernel(
    stages,
    q_hbm, k_hbm, v_hbm, c_hbm, count_hbm, trades_hbm, scale_hbm,
    att_final, dq, dk, dv, sum_out,
    q, k, v, own_c, c_first, c_send, c_second, cot,
    att, a_first, a_send, a_second,
    weights, mixed, part, sum_recv, scale_ref, count_ref, trades_ref,
    load_sem, send_sem, recv_sem, sum_send_sem, sum_recv_sem, ready,
):
    g = lax.axis_index("group")
    d = lax.axis_index("dp")
    length, width = q.shape
    pairs = width // LANES
    half = length // 2
    rows = half // PARTS

    def peer(moves):
        pg, pd = g, d
        for axis, bit in moves:
            if axis == "group":
                pg = flip(pg, bit)
            else:
                pd = flip(pd, bit)
        return (pd, pg)

    def upper_half(move):
        axis, bit = move
        return ((g if axis == "group" else d) // bit) % 2 == 1

    def rank(pd, pg):
        size = 2 ** sum(axis == "dp" for stage in stages for axis, _ in stage)
        ny = size // 4
        z, x = pd // (size // 2) * 4 + pg // 4, pg % 4
        y, core = (pd // 2) % ny, pd % 2
        y = jnp.where(2 * y < ny, y, ny // 2 + ny - 1 - y)
        place = 2 * (((z * ny + y) * 4 + x) * 2 + 1 - core)
        return jnp.where(pd + pg == 0, 64 * ny - 1, place)

    def upper(moves):
        return rank(d, g) > rank(*peer(moves))

    loads = [
        pltpu.make_async_copy(src, dst, load_sem.at[i])
        for i, (src, dst) in enumerate([
            (q_hbm.at[0], q), (k_hbm.at[0], k), (v_hbm.at[0], v), (c_hbm.at[0], own_c),
            (count_hbm, count_ref), (trades_hbm, trades_ref), (scale_hbm, scale_ref),
        ])
    ]

    meetings = [moves for stage in stages for moves in stage_moves(stage)]
    meetings.sort(key=lambda moves: moves not in ([("group", NEAR)], [("group", FAR)]))
    barrier = pltpu.get_barrier_semaphore()
    greetings = 0
    for moves in meetings:
        greetings = greetings + upper(moves).astype(jnp.int32)

        @pl.when(jnp.logical_not(upper(moves)))
        def _(moves=moves):
            pl.semaphore_signal(barrier, inc=1, device_id=peer(moves), device_id_type=MESH)

    @pl.when(greetings > 0)
    def _():
        pl.semaphore_wait(barrier, greetings)

    for j, moves in enumerate(meetings):

        @pl.when(upper(moves))
        def _(j=j, moves=moves):
            pl.semaphore_signal(ready.at[j], inc=1, device_id=peer(moves), device_id_type=MESH)

    met = []

    def meet(moves):
        j = meetings.index(moves)
        if j in met:
            return
        met.append(j)

        @pl.when(jnp.logical_not(upper(moves)))
        def _():
            pl.semaphore_wait(ready.at[j], 1)

    def spans(part_index):
        return pl.ds(part_index * rows, rows), pl.ds(half + part_index * rows, rows)

    def remote(src, dst, bit, slot):
        return pltpu.make_async_remote_copy(
            src_ref=src, dst_ref=dst, send_sem=send_sem.at[slot], recv_sem=recv_sem.at[slot],
            device_id=peer([("group", bit)]), device_id_type=MESH,
        )

    c_hop1, c_hop2, a_hop1, a_hop2 = [], [], [], []
    for i in range(PARTS):
        top, low = spans(i)
        c_hop1.append((
            remote(c_hbm.at[0, top], c_first.at[top], NEAR, 8 * i),
            remote(c_hbm.at[0, low], c_first.at[low], FAR, 8 * i + 1),
        ))
        c_hop2.append((
            remote(c_send.at[top], c_second.at[top], FAR, 8 * i + 2),
            remote(c_send.at[low], c_second.at[low], NEAR, 8 * i + 3),
        ))
        a_hop1.append((
            remote(att.at[top], a_first.at[top], FAR, 8 * i + 4),
            remote(att.at[low], a_first.at[low], NEAR, 8 * i + 5),
        ))
        a_hop2.append((
            remote(a_send.at[top], a_second.at[top], NEAR, 8 * i + 6),
            remote(a_send.at[low], a_second.at[low], FAR, 8 * i + 7),
        ))

    def start(hop):
        for copy in hop:
            copy.start()

    def pick(chosen, other, pred):
        return lax.select(pred, chosen, other)

    def c_turn(i):
        top, low = spans(i)
        c_hop1[i][0].wait_recv()
        c_send[top] = pick(c_first[top], own_c[top], near_mine)
        c_hop2[i][0].start()
        c_hop1[i][1].wait_recv()
        c_send[low] = pick(c_first[low], own_c[low], far_other)
        c_hop2[i][1].start()

    def c_land(i):
        top, low = spans(i)
        c_hop2[i][0].wait_recv()
        cot[top] = pick(c_second[top], c_send[top], far_mine)
        c_hop2[i][1].wait_recv()
        cot[low] = pick(c_second[low], pick(c_first[low], own_c[low], far_mine), near_at_source)

    def a_turn(i):
        top, low = spans(i)
        a_hop1[i][0].wait_recv()
        a_send[top] = pick(a_first[top], att[top], far_mine)
        a_hop2[i][0].start()
        a_hop1[i][1].wait_recv()
        a_send[low] = pick(a_first[low], att[low], near_other)
        a_hop2[i][1].start()

    def a_land(i):
        top, low = spans(i)
        a_hop2[i][0].wait_recv()
        att_final[0, top] = pick(a_second[top], a_send[top], near_mine)
        a_hop2[i][1].wait_recv()
        att_final[0, low] = pick(a_second[low], pick(a_first[low], att[low], near_mine), far_at_source)

    def sum_copies(s):
        return [
            pltpu.make_async_remote_copy(
                src_ref=part.at[s], dst_ref=sum_recv.at[s, j],
                send_sem=sum_send_sem.at[7 * s + j], recv_sem=sum_recv_sem.at[7 * s + j],
                device_id=peer(moves), device_id_type=MESH,
            )
            for j, moves in enumerate(stage_moves(stages[s]))
        ]

    def sum_start(s):
        for moves in stage_moves(stages[s]):
            meet(moves)
        for copy in sum_copies(s):
            copy.start()

    def sum_finish(s):
        for copy in sum_copies(s):
            copy.wait_recv()
        terms = [part[s]] + [sum_recv[s, j] for j in range(len(stage_moves(stages[s])))]
        while len(terms) > 1:
            terms = [terms[i] + terms[i + 1] for i in range(0, len(terms), 2)]
        if s + 1 < len(stages):
            part[s + 1] = terms[0]
            sum_start(s + 1)
        else:
            sum_out[...] = terms[0][: width // LANES]

    meet([("group", NEAR)])
    c_hop1[0][0].start()
    meet([("group", FAR)])
    c_hop1[0][1].start()
    for i in range(1, PARTS):
        start(c_hop1[i])
    for copy in loads:
        copy.start()
    for copy in loads:
        copy.wait()

    a, b, x = g // 8, (g // 4) % 2, g % 4
    base = d * 16 + x

    def flag(offset, round_index):
        return trades_ref[round_index, base + offset] == 1

    far_mine, far_other = flag(b * 4, 0), flag((1 - b) * 4, 0)
    near_mine, near_other = flag(a * 8, 1), flag((1 - a) * 8, 1)
    near_at_source = jnp.logical_or(
        jnp.logical_and(far_mine, near_other),
        jnp.logical_and(jnp.logical_not(far_mine), near_mine),
    )
    far_at_source = jnp.logical_or(
        jnp.logical_and(near_mine, far_other),
        jnp.logical_and(jnp.logical_not(near_mine), far_mine),
    )

    total_rows = count_ref[0] + 4
    key_bias = jnp.where(
        lax.broadcasted_iota(jnp.int32, (1, length), 1) < total_rows, 0.0, -jnp.inf
    ).astype(F32)

    def columns(pair):
        return pl.ds(pl.multiple_of(pair * LANES, LANES), LANES)

    def halves(block):
        lane = lax.broadcasted_iota(jnp.int32, block.shape, 1)
        wide = block.astype(F32)
        return (
            jnp.where(lane < HEAD_DIM, wide, 0.0).astype(BF16),
            jnp.where(lane < HEAD_DIM, 0.0, wide).astype(BF16),
        )

    def row_valid():
        return lax.broadcasted_iota(jnp.int32, (length, LANES), 0) < total_rows

    def forward(pair, carry):
        cols = columns(pair)
        keys = k[:, cols]
        blend = None
        for j, (q_half, v_half) in enumerate(zip(halves(q[:, cols]), halves(v[:, cols]))):
            scores = nt_dot(q_half, keys) + key_bias
            top = jnp.max(scores, axis=1, keepdims=True)
            expd = jnp.exp2((scores - top) * EXP_SCALE)
            low = (expd * (1.0 / jnp.sum(expd, axis=1, keepdims=True))).astype(BF16)
            weights[2 * pair + j] = low
            term = nn_dot(low, v_half)
            blend = term if blend is None else blend + term
        mixed_low = blend.astype(BF16)
        mixed[:, cols] = mixed_low
        out = jnp.where(row_valid(), scale_ref[pl.ds(pair, 1), :] * mixed_low.astype(F32), 0.0)
        att[:, cols] = out.astype(BF16)
        return carry

    def scale_rows(begin):
        valid = begin + lax.broadcasted_iota(jnp.int32, (rows, LANES), 0) < total_rows
        for pair in range(pairs):
            cols = pl.ds(pair * LANES, LANES)
            span = pl.ds(begin, rows)
            product = cot[span, cols].astype(F32) * mixed[span, cols].astype(F32)
            part[0, pl.ds(pair, 1), :] += jnp.sum(
                jnp.where(valid, product, 0.0), axis=0, keepdims=True
            )

    def backward(pair, carry):
        cols = columns(pair)
        up = jnp.where(row_valid(), cot[:, cols].astype(F32) * scale_ref[pl.ds(pair, 1), :], 0.0)
        values = v[:, cols]
        blended = mixed[:, cols].astype(F32)
        dq_sum = dk_sum = dv_sum = None
        parts = zip(halves(up), halves(k[:, cols]), halves(q[:, cols]))
        for j, (up_half, k_half, q_half) in enumerate(parts):
            low = weights[2 * pair + j]
            delta = jnp.sum(up_half.astype(F32) * blended, axis=1, keepdims=True)
            grad = (low.astype(F32) * (nt_dot(up_half, values) - delta)).astype(BF16)
            dq_term, dk_term, dv_term = nn_dot(grad, k_half), tn_dot(grad, q_half), tn_dot(low, up_half)
            dq_sum = dq_term if j == 0 else dq_sum + dq_term
            dk_sum = dk_term if j == 0 else dk_sum + dk_term
            dv_sum = dv_term if j == 0 else dv_sum + dv_term
        dq[0, :, cols] = (dq_sum * FACTOR).astype(BF16)
        dk[0, :, cols] = (dk_sum * FACTOR).astype(BF16)
        dv[0, :, cols] = dv_sum.astype(BF16)
        return carry

    lax.fori_loop(0, pairs // 2, forward, 0)
    c_turn(0)
    lax.fori_loop(pairs // 2, pairs, forward, 0)
    for i in range(1, PARTS):
        c_turn(i)
    late = jnp.logical_or(upper_half(stages[0][0]), upper_half(("group", FAR)))
    start(a_hop1[0])

    @pl.when(jnp.logical_not(late))
    def _():
        for i in range(1, PARTS):
            start(a_hop1[i])

    part[0] = jnp.zeros((8, LANES), F32)
    for i in range(PARTS):
        c_land(i)
        scale_rows(i * rows)
        scale_rows(half + i * rows)
    sum_start(0)

    @pl.when(late)
    def _():
        for i in range(1, PARTS):
            start(a_hop1[i])

    lax.fori_loop(0, pairs // 2, backward, 0)
    a_turn(0)
    lax.fori_loop(pairs // 2, pairs, backward, 0)
    for i in range(1, PARTS):
        a_turn(i)
    for s in range(len(stages) - 1):
        sum_finish(s)
    for i in range(PARTS - 1):
        a_land(i)
    sum_finish(len(stages) - 1)
    a_land(PARTS - 1)
    for i in range(PARTS):
        for hop in (c_hop1[i], c_hop2[i], a_hop1[i], a_hop2[i]):
            for copy in hop:
                copy.wait_send()
    for s in range(len(stages)):
        for copy in sum_copies(s):
            copy.wait_send()


def settle(*refs):
    half = len(refs) // 2
    sources, results, sem = refs[:half], refs[half:-1], refs[-1]
    copies = [
        pltpu.make_async_copy(src, dst, sem.at[i])
        for i, (src, dst) in enumerate(zip(sources, results))
    ]
    for copy in copies:
        copy.start()
    for copy in copies:
        copy.wait()


def per_device(stages, query_rows, key_rows, value_rows, cotangent, kept_counts, trades, layer_scale):
    _, length, width = query_rows.shape
    heads = width // HEAD_DIM
    tiles = width // LANES
    block = pltpu.VMEM((length, width), BF16)
    image = pltpu.VMEM((1, length, width), BF16)
    hbm = pl.BlockSpec(memory_space=pl.ANY)
    vmem = pl.BlockSpec(memory_space=pltpu.VMEM)
    slots = 8 * PARTS
    meetings = sum(len(stage_moves(stage)) for stage in stages)
    results = pl.pallas_call(
        functools.partial(kernel, stages),
        out_shape=(image, image, image, image, pltpu.VMEM((tiles, LANES), F32)),
        in_specs=[hbm] * 7,
        out_specs=(vmem,) * 5,
        scratch_shapes=[
            *[block] * 12,
            pltpu.VMEM((heads, length, length), BF16),
            block,
            pltpu.VMEM((len(stages), 8, LANES), F32),
            pltpu.VMEM((len(stages), 7, 8, LANES), F32),
            pltpu.VMEM((tiles, LANES), F32),
            pltpu.SMEM((1,), jnp.int32),
            pltpu.SMEM(trades.shape[::-1], jnp.int32),
            pltpu.SemaphoreType.DMA((7,)),
            pltpu.SemaphoreType.DMA((slots,)),
            pltpu.SemaphoreType.DMA((slots,)),
            pltpu.SemaphoreType.DMA((7 * len(stages),)),
            pltpu.SemaphoreType.DMA((7 * len(stages),)),
            pltpu.SemaphoreType.REGULAR((meetings,)),
        ],
        compiler_params=pltpu.CompilerParams(
            collective_id=0, has_side_effects=True, vmem_limit_bytes=52 * 2**20
        ),
        cost_estimate=pl.CostEstimate(
            flops=12 * heads * length * length * HEAD_DIM,
            bytes_accessed=16 * length * width,
            transcendentals=heads * length * length,
        ),
    )(
        query_rows, key_rows, value_rows, cotangent,
        kept_counts, trades.T, layer_scale.reshape(tiles, LANES),
    )
    attended, query_grad, key_grad, value_grad, scale_sum = pl.pallas_call(
        settle,
        out_shape=tuple(jax.ShapeDtypeStruct(item.shape, item.dtype) for item in results),
        in_specs=[hbm] * 5,
        out_specs=(hbm,) * 5,
        scratch_shapes=[pltpu.SemaphoreType.DMA((5,))],
        compiler_params=pltpu.CompilerParams(vmem_limit_bytes=2**20),
    )(*results)
    return attended, query_grad, key_grad, value_grad, scale_sum.reshape(width)


def solution(mesh):
    rows = P(("dp", "group"), None, None)
    return jax.shard_map(
        functools.partial(per_device, sum_stages(mesh.shape["dp"])),
        mesh=mesh,
        in_specs=(rows, rows, rows, rows, P(("dp", "group")), P(), P()),
        out_specs=(rows, rows, rows, rows, P()),
        check_vma=False,
    )
```

```python
import functools
import math

import jax
import jax.numpy as jnp
from jax import lax
from jax.experimental import pallas as pl
from jax.experimental.pallas import tpu as pltpu
from jax.sharding import PartitionSpec as P

MESH = pl.DeviceIdType.MESH
BF16 = jnp.bfloat16
F32 = jnp.float32
HEAD_DIM = 64
LANES = 128
FACTOR = HEAD_DIM ** -0.5
EXP_SCALE = FACTOR * math.log2(math.e)
PARTS = 4

NEAR, FAR = 4, 8


def flip(index, bit):
    return index + bit * (1 - 2 * ((index // bit) % 2))


def nt_dot(a, b):
    return lax.dot_general(a, b, (((1,), (1,)), ((), ())), preferred_element_type=F32)


def tn_dot(a, b):
    return lax.dot_general(a, b, (((0,), (0,)), ((), ())), preferred_element_type=F32)


def nn_dot(a, b):
    return jnp.dot(a, b, preferred_element_type=F32)


def sum_stages(dp_size):
    top = dp_size // 2
    middle, bit = [], 2
    while bit < top:
        middle.insert(0, ("dp", bit))
        bit *= 2
    stages = [
        [("dp", top), ("group", FAR), ("group", NEAR)], [("group", 2), ("group", 1), ("dp", 1)], middle
    ]
    return [stage for stage in stages if stage]


def stage_moves(stage):
    count = len(stage)
    return [
        [stage[i] for i in range(count) if choice >> (count - 1 - i) & 1]
        for choice in range(1, 2**count)
    ]


def kernel(
    stages,
    q_hbm, k_hbm, v_hbm, c_hbm, count_hbm, trades_hbm, scale_hbm,
    att_final, dq, dk, dv, sum_out,
    q, k, v, own_c, c_first, c_send, c_second, cot,
    att, a_first, a_send, a_second,
    weights, mixed, part, sum_recv, scale_ref, count_ref, trades_ref,
    load_sem, send_sem, recv_sem, sum_send_sem, sum_recv_sem, ready,
):
    g = lax.axis_index("group")
    d = lax.axis_index("dp")
    length, width = q.shape
    pairs = width // LANES
    half = length // 2
    rows = half // PARTS

    def peer(moves):
        pg, pd = g, d
        for axis, bit in moves:
            if axis == "group":
                pg = flip(pg, bit)
            else:
                pd = flip(pd, bit)
        return (pd, pg)

    def upper_half(move):
        axis, bit = move
        return ((g if axis == "group" else d) // bit) % 2 == 1

    def rank(pd, pg):
        size = 2 ** sum(axis == "dp" for stage in stages for axis, _ in stage)
        ny = size // 4
        z, x = pd // (size // 2) * 4 + pg // 4, pg % 4
        y, core = (pd // 2) % ny, pd % 2
        y = jnp.where(2 * y < ny, y, ny // 2 + ny - 1 - y)
        place = 2 * (((z * ny + y) * 4 + x) * 2 + 1 - core)
        return jnp.where(pd + pg == 0, 64 * ny - 1, place)

    def upper(moves):
        return rank(d, g) > rank(*peer(moves))

    loads = [
        pltpu.make_async_copy(src, dst, load_sem.at[i])
        for i, (src, dst) in enumerate([
            (q_hbm.at[0], q), (k_hbm.at[0], k), (v_hbm.at[0], v), (c_hbm.at[0], own_c),
            (count_hbm, count_ref), (trades_hbm, trades_ref), (scale_hbm, scale_ref),
        ])
    ]

    meetings = [moves for stage in stages for moves in stage_moves(stage)]
    meetings.sort(key=lambda moves: moves not in ([("group", NEAR)], [("group", FAR)]))
    barrier = pltpu.get_barrier_semaphore()
    greetings = 0
    for moves in meetings:
        greetings = greetings + upper(moves).astype(jnp.int32)

        @pl.when(jnp.logical_not(upper(moves)))
        def _(moves=moves):
            pl.semaphore_signal(barrier, inc=1, device_id=peer(moves), device_id_type=MESH)

    @pl.when(greetings > 0)
    def _():
        pl.semaphore_wait(barrier, greetings)

    def answer(j):
        @pl.when(upper(meetings[j]))
        def _():
            pl.semaphore_signal(
                ready.at[j], inc=1, device_id=peer(meetings[j]), device_id_type=MESH
            )

    answer(0)
    answer(1)
    met = []

    def meet(moves):
        j = meetings.index(moves)
        if j in met:
            return
        met.append(j)

        @pl.when(jnp.logical_not(upper(moves)))
        def _():
            pl.semaphore_wait(ready.at[j], 1)

    def spans(part_index):
        return pl.ds(part_index * rows, rows), pl.ds(half + part_index * rows, rows)

    def remote(src, dst, bit, slot):
        return pltpu.make_async_remote_copy(
            src_ref=src, dst_ref=dst, send_sem=send_sem.at[slot], recv_sem=recv_sem.at[slot],
            device_id=peer([("group", bit)]), device_id_type=MESH,
        )

    c_hop1, c_hop2, a_hop1, a_hop2 = [], [], [], []
    for i in range(PARTS):
        top, low = spans(i)
        c_hop1.append((
            remote(c_hbm.at[0, top], c_first.at[top], NEAR, 8 * i),
            remote(c_hbm.at[0, low], c_first.at[low], FAR, 8 * i + 1),
        ))
        c_hop2.append((
            remote(c_send.at[top], c_second.at[top], FAR, 8 * i + 2),
            remote(c_send.at[low], c_second.at[low], NEAR, 8 * i + 3),
        ))
        a_hop1.append((
            remote(att.at[top], a_first.at[top], FAR, 8 * i + 4),
            remote(att.at[low], a_first.at[low], NEAR, 8 * i + 5),
        ))
        a_hop2.append((
            remote(a_send.at[top], a_second.at[top], NEAR, 8 * i + 6),
            remote(a_send.at[low], a_second.at[low], FAR, 8 * i + 7),
        ))

    def start(hop):
        for copy in hop:
            copy.start()

    def pick(chosen, other, pred):
        return lax.select(pred, chosen, other)

    def c_turn(i):
        top, low = spans(i)
        c_hop1[i][0].wait_recv()
        c_send[top] = pick(c_first[top], own_c[top], near_mine)
        c_hop2[i][0].start()
        c_hop1[i][1].wait_recv()
        c_send[low] = pick(c_first[low], own_c[low], far_other)
        c_hop2[i][1].start()

    def c_land(i):
        top, low = spans(i)
        c_hop2[i][0].wait_recv()
        cot[top] = pick(c_second[top], c_send[top], far_mine)
        c_hop2[i][1].wait_recv()
        cot[low] = pick(c_second[low], pick(c_first[low], own_c[low], far_mine), near_at_source)

    def a_turn(i):
        top, low = spans(i)
        a_hop1[i][0].wait_recv()
        a_send[top] = pick(a_first[top], att[top], far_mine)
        a_hop2[i][0].start()
        a_hop1[i][1].wait_recv()
        a_send[low] = pick(a_first[low], att[low], near_other)
        a_hop2[i][1].start()

    def a_land(i):
        top, low = spans(i)
        a_hop2[i][0].wait_recv()
        att_final[0, top] = pick(a_second[top], a_send[top], near_mine)
        a_hop2[i][1].wait_recv()
        att_final[0, low] = pick(a_second[low], pick(a_first[low], att[low], near_mine), far_at_source)

    def sum_copies(s):
        return [
            pltpu.make_async_remote_copy(
                src_ref=part.at[s], dst_ref=sum_recv.at[s, j],
                send_sem=sum_send_sem.at[7 * s + j], recv_sem=sum_recv_sem.at[7 * s + j],
                device_id=peer(moves), device_id_type=MESH,
            )
            for j, moves in enumerate(stage_moves(stages[s]))
        ]

    def sum_start(s):
        for moves in stage_moves(stages[s]):
            meet(moves)
        for copy in sum_copies(s):
            copy.start()

    def sum_finish(s):
        for copy in sum_copies(s):
            copy.wait_recv()
        terms = [part[s]] + [sum_recv[s, j] for j in range(len(stage_moves(stages[s])))]
        while len(terms) > 1:
            terms = [terms[i] + terms[i + 1] for i in range(0, len(terms), 2)]
        if s + 1 < len(stages):
            part[s + 1] = terms[0]
            sum_start(s + 1)
        else:
            sum_out[...] = terms[0][: width // LANES]

    meet([("group", NEAR)])
    c_hop1[0][0].start()
    meet([("group", FAR)])
    c_hop1[0][1].start()
    for i in range(1, PARTS):
        start(c_hop1[i])
    for copy in loads:
        copy.start()
    for j in range(2, len(meetings)):
        answer(j)
    for copy in loads:
        copy.wait()

    a, b, x = g // 8, (g // 4) % 2, g % 4
    base = d * 16 + x

    def flag(offset, round_index):
        return trades_ref[round_index, base + offset] == 1

    far_mine, far_other = flag(b * 4, 0), flag((1 - b) * 4, 0)
    near_mine, near_other = flag(a * 8, 1), flag((1 - a) * 8, 1)
    near_at_source = jnp.logical_or(
        jnp.logical_and(far_mine, near_other),
        jnp.logical_and(jnp.logical_not(far_mine), near_mine),
    )
    far_at_source = jnp.logical_or(
        jnp.logical_and(near_mine, far_other),
        jnp.logical_and(jnp.logical_not(near_mine), far_mine),
    )

    total_rows = count_ref[0] + 4
    key_bias = jnp.where(
        lax.broadcasted_iota(jnp.int32, (1, length), 1) < total_rows, 0.0, -jnp.inf
    ).astype(F32)

    def columns(pair):
        return pl.ds(pl.multiple_of(pair * LANES, LANES), LANES)

    def halves(block):
        lane = lax.broadcasted_iota(jnp.int32, block.shape, 1)
        wide = block.astype(F32)
        return (
            jnp.where(lane < HEAD_DIM, wide, 0.0).astype(BF16),
            jnp.where(lane < HEAD_DIM, 0.0, wide).astype(BF16),
        )

    def row_valid():
        return lax.broadcasted_iota(jnp.int32, (length, LANES), 0) < total_rows

    def forward(pair, carry):
        cols = columns(pair)
        keys = k[:, cols]
        blend = None
        for j, (q_half, v_half) in enumerate(zip(halves(q[:, cols]), halves(v[:, cols]))):
            scores = nt_dot(q_half, keys) + key_bias
            top = jnp.max(scores, axis=1, keepdims=True)
            expd = jnp.exp2((scores - top) * EXP_SCALE)
            low = (expd * (1.0 / jnp.sum(expd, axis=1, keepdims=True))).astype(BF16)
            weights[2 * pair + j] = low
            term = nn_dot(low, v_half)
            blend = term if blend is None else blend + term
        mixed_low = blend.astype(BF16)
        mixed[:, cols] = mixed_low
        out = jnp.where(row_valid(), scale_ref[pl.ds(pair, 1), :] * mixed_low.astype(F32), 0.0)
        att[:, cols] = out.astype(BF16)
        return carry

    def scale_rows(begin):
        valid = begin + lax.broadcasted_iota(jnp.int32, (rows, LANES), 0) < total_rows
        for pair in range(pairs):
            cols = pl.ds(pair * LANES, LANES)
            span = pl.ds(begin, rows)
            product = cot[span, cols].astype(F32) * mixed[span, cols].astype(F32)
            part[0, pl.ds(pair, 1), :] += jnp.sum(
                jnp.where(valid, product, 0.0), axis=0, keepdims=True
            )

    def backward(pair, carry):
        cols = columns(pair)
        up = jnp.where(row_valid(), cot[:, cols].astype(F32) * scale_ref[pl.ds(pair, 1), :], 0.0)
        values = v[:, cols]
        blended = mixed[:, cols].astype(F32)
        dq_sum = dk_sum = dv_sum = None
        parts = zip(halves(up), halves(k[:, cols]), halves(q[:, cols]))
        for j, (up_half, k_half, q_half) in enumerate(parts):
            low = weights[2 * pair + j]
            delta = jnp.sum(up_half.astype(F32) * blended, axis=1, keepdims=True)
            grad = (low.astype(F32) * (nt_dot(up_half, values) - delta)).astype(BF16)
            dq_term, dk_term, dv_term = nn_dot(grad, k_half), tn_dot(grad, q_half), tn_dot(low, up_half)
            dq_sum = dq_term if j == 0 else dq_sum + dq_term
            dk_sum = dk_term if j == 0 else dk_sum + dk_term
            dv_sum = dv_term if j == 0 else dv_sum + dv_term
        dq[0, :, cols] = (dq_sum * FACTOR).astype(BF16)
        dk[0, :, cols] = (dk_sum * FACTOR).astype(BF16)
        dv[0, :, cols] = dv_sum.astype(BF16)
        return carry

    lax.fori_loop(0, pairs // 2, forward, 0)
    c_turn(0)
    lax.fori_loop(pairs // 2, pairs, forward, 0)
    for i in range(1, PARTS):
        c_turn(i)
    late = jnp.logical_or(upper_half(stages[0][0]), upper_half(("group", FAR)))
    start(a_hop1[0])

    @pl.when(jnp.logical_not(late))
    def _():
        for i in range(1, PARTS):
            start(a_hop1[i])

    part[0] = jnp.zeros((8, LANES), F32)
    for i in range(PARTS):
        c_land(i)
        scale_rows(i * rows)
        scale_rows(half + i * rows)
    sum_start(0)

    @pl.when(late)
    def _():
        for i in range(1, PARTS):
            start(a_hop1[i])

    lax.fori_loop(0, pairs // 2, backward, 0)
    a_turn(0)
    lax.fori_loop(pairs // 2, pairs, backward, 0)
    for i in range(1, PARTS):
        a_turn(i)
    for s in range(len(stages) - 1):
        sum_finish(s)
    for i in range(PARTS - 1):
        a_land(i)
    sum_finish(len(stages) - 1)

    sent = [copy for i in range(PARTS) for hop in (c_hop1[i], c_hop2[i], a_hop1[i]) for copy in hop]
    sent += [copy for s in range(len(stages)) for copy in sum_copies(s)]
    sent += [copy for hop in a_hop2[:-1] for copy in hop]
    for copy in sent:
        copy.wait_send()
    a_land(PARTS - 1)
    for copy in a_hop2[-1]:
        copy.wait_send()


def settle(*refs):
    half = len(refs) // 2
    sources, results, sem = refs[:half], refs[half:-1], refs[-1]
    copies = [
        pltpu.make_async_copy(src, dst, sem.at[i])
        for i, (src, dst) in enumerate(zip(sources, results))
    ]
    for copy in copies:
        copy.start()
    for copy in copies:
        copy.wait()


def per_device(stages, query_rows, key_rows, value_rows, cotangent, kept_counts, trades, layer_scale):
    _, length, width = query_rows.shape
    heads = width // HEAD_DIM
    tiles = width // LANES
    block = pltpu.VMEM((length, width), BF16)
    image = pltpu.VMEM((1, length, width), BF16)
    hbm = pl.BlockSpec(memory_space=pl.ANY)
    vmem = pl.BlockSpec(memory_space=pltpu.VMEM)
    slots = 8 * PARTS
    meetings = sum(len(stage_moves(stage)) for stage in stages)
    results = pl.pallas_call(
        functools.partial(kernel, stages),
        out_shape=(image, image, image, image, pltpu.VMEM((tiles, LANES), F32)),
        in_specs=[hbm] * 7,
        out_specs=(vmem,) * 5,
        scratch_shapes=[
            *[block] * 12,
            pltpu.VMEM((heads, length, length), BF16),
            block,
            pltpu.VMEM((len(stages), 8, LANES), F32),
            pltpu.VMEM((len(stages), 7, 8, LANES), F32),
            pltpu.VMEM((tiles, LANES), F32),
            pltpu.SMEM((1,), jnp.int32),
            pltpu.SMEM(trades.shape[::-1], jnp.int32),
            pltpu.SemaphoreType.DMA((7,)),
            pltpu.SemaphoreType.DMA((slots,)),
            pltpu.SemaphoreType.DMA((slots,)),
            pltpu.SemaphoreType.DMA((7 * len(stages),)),
            pltpu.SemaphoreType.DMA((7 * len(stages),)),
            pltpu.SemaphoreType.REGULAR((meetings,)),
        ],
        compiler_params=pltpu.CompilerParams(
            collective_id=0, has_side_effects=True, vmem_limit_bytes=52 * 2**20
        ),
        cost_estimate=pl.CostEstimate(
            flops=12 * heads * length * length * HEAD_DIM,
            bytes_accessed=16 * length * width,
            transcendentals=heads * length * length,
        ),
    )(
        query_rows, key_rows, value_rows, cotangent,
        kept_counts, trades.T, layer_scale.reshape(tiles, LANES),
    )
    attended, query_grad, key_grad, value_grad, scale_sum = pl.pallas_call(
        settle,
        out_shape=tuple(jax.ShapeDtypeStruct(item.shape, item.dtype) for item in results),
        in_specs=[hbm] * 5,
        out_specs=(hbm,) * 5,
        scratch_shapes=[pltpu.SemaphoreType.DMA((5,))],
        compiler_params=pltpu.CompilerParams(vmem_limit_bytes=2**20),
    )(*results)
    return attended, query_grad, key_grad, value_grad, scale_sum.reshape(width)


def solution(mesh):
    rows = P(("dp", "group"), None, None)
    return jax.shard_map(
        functools.partial(per_device, sum_stages(mesh.shape["dp"])),
        mesh=mesh,
        in_specs=(rows, rows, rows, rows, P(("dp", "group")), P(), P()),
        out_specs=(rows, rows, rows, rows, P()),
        check_vma=False,
    )
```
